32 devices in a mesh: slab: 4 (over x, core), wide: 8 (over z, y).
Axes of the slice: x: 2, y: 2, z: 4, core: 2. Of those that a mesh axis runs over, the one named last changes fastest.
Arguments:
- orbitals: float32 [256, 128, 128, 128], P(None, 'slab', 'wide'), may hold values from -6 to 6
- points: int32 [512], replicated, may hold values from 0 to 2097151, as said below
Outputs:
- potential: float32 [32, 128, 128, 128], P(None, 'slab', 'wide')
The draws below stay inside these ranges and needn't reach their ends.
Inputs may be any that keep to these rules, and one draw needn't show every extreme that they name: `points`: the 512 indices are distinct; how many fall in the cells of one device differs strongly between devices.
All inputs are finite; a program needn't handle non-finite values.
Results may differ from the reference program's by a relative error of at most 0.00014.
Values sent between devices are 32-bit elements; how exact they have to be, the bound alone decides.
A program may use at most 256 MiB of HBM per device.

```python
import math
import jax
import jax.numpy as jnp
from jax import lax

NG = 128
ORB = 256
NPTS = 512
VEC = 32
CZ = 32
CY = 16
CELLS = 65536


def draw_points(key, part):
    first, second = jax.random.split(key, 2)
    wide_count = NG // CY
    device_count = NG // CZ * wide_count
    factors = jax.random.randint(first, (2, NPTS - 2), 0, device_count)
    owner = factors[0] * factors[1] // device_count
    owner = jnp.concatenate([jnp.array([device_count - 1, 0], jnp.int32), owner.astype(jnp.int32)])
    shuffled = jax.random.permutation(second, CELLS - 2)[:NPTS - 2] + 1
    offset = jnp.concatenate([jnp.array([CELLS - 1, 0], jnp.int32), shuffled.astype(jnp.int32)])
    slab_pos = owner // wide_count
    wide_pos = owner % wide_count
    local_z = offset // (CY * NG)
    local_y = offset // NG % CY
    local_x = offset % NG
    zcoord = slab_pos * CZ + local_z
    ycoord = wide_pos * CY + local_y
    return ((zcoord * NG + ycoord) * NG + local_x).astype(jnp.int32)


def level_of(own_key, dims, cuts, least, largest):
    loudness, own = 1.0, jax.random.fold_in(own_key, 6)
    for axis_at, shards_of in cuts:
        steps = jnp.exp(jax.random.uniform(jax.random.fold_in(own, axis_at), (shards_of,), jnp.float32, least / len(cuts), largest / len(cuts)))
        loudness = loudness * jnp.repeat(steps, dims[axis_at] // shards_of).reshape([-1 if axis == axis_at else 1 for axis in range(len(dims))])
    return loudness


def normal_values(key, dims, spread, most, cuts=(), kind=jnp.bfloat16):
    values = spread * jax.random.normal(key, dims, jnp.float32)
    if cuts:
        values = values * level_of(key, dims, cuts, -0.22, 0.18)
    return jnp.clip(values, -most, most).astype(kind)


def setup_inputs(seed: int = 0) -> dict:
    arg_keys = jax.random.split(jax.random.key(seed), 3)
    orbitals = normal_values(arg_keys[0], (ORB, NG, NG, NG), 1.0, 6.0, ((1, 4), (2, 8)), jnp.float32)
    points = draw_points(jax.random.fold_in(arg_keys[2], 71), 0)
    return {"orbitals": orbitals, "points": points}


highest = lax.Precision.HIGHEST

def coulomb(zfreq, yfreq, xfreq, length, factor):

    def squared(index):
        signed = jnp.where(index > length // 2, index - length, index).astype(jnp.float32) * (2.0 * math.pi / length)
        return signed * signed
    total = squared(zfreq)[:, None, None] + squared(yfreq)[None, :, None] + squared(xfreq)[None, None, :]
    safe = jnp.where(total > 0, total, 1.0)
    return jnp.where(total > 0, 4.0 * math.pi * factor / safe, 0.0)

def reference(orbitals, points):
    flat = orbitals.reshape(ORB, NG * NG * NG)
    sampled = jnp.take(flat, points, axis=1)
    correlation = jnp.dot(sampled.T, sampled, precision=highest)
    gram = correlation * correlation
    gram = gram + 0.01 * jnp.mean(jnp.diagonal(gram)) * jnp.eye(NPTS, dtype=jnp.float32)
    factor = jnp.linalg.cholesky(gram)
    coeffs = jax.scipy.linalg.cho_solve((factor, True), jnp.eye(NPTS, VEC, dtype=jnp.float32))

    def plane_fit(zindex):
        block = lax.dynamic_slice_in_dim(orbitals, zindex, 1, axis=1).reshape(ORB, NG * NG)
        pairs = jnp.dot(sampled.T, block, precision=highest)
        return jnp.dot(coeffs.T, pairs * pairs, precision=highest)
    fitted = lax.map(plane_fit, jnp.arange(NG, dtype=jnp.int32))
    fitting = jnp.transpose(fitted, (1, 0, 2)).reshape(VEC, NG, NG, NG)
    freqs = jnp.arange(NG, dtype=jnp.int32)
    kernel = coulomb(freqs, freqs, freqs, NG, 1.0)
    spectrum = jnp.fft.fftn(fitting, axes=(1, 2, 3))
    return jnp.real(jnp.fft.ifftn(spectrum * kernel, axes=(1, 2, 3))).astype(jnp.float32)
```

```python
import functools
import math

import jax
import jax.numpy as jnp
import ml_dtypes
import numpy as np
from jax import lax
from jax.experimental import pallas as pl
from jax.experimental.pallas import tpu as pltpu
from jax.sharding import PartitionSpec as P

highest = lax.Precision.HIGHEST
MESH = pl.DeviceIdType.MESH
MIB = 1 << 20
f32 = jnp.float32
bf16 = jnp.bfloat16


def split(values):
    high = values.astype(bf16)
    low = (values - high.astype(f32)).astype(bf16)
    return high, low


def mul(left, right):
    return jnp.dot(left, right, preferred_element_type=f32)


def pick_kernel(slots, code_ref, orb_ref, out_ref, owned_ref, buf, sem):
    npoint, norbit = out_ref.shape
    grid = orb_ref.shape[-1]
    out_ref[...] = jnp.zeros_like(out_ref)

    def scan(point, count):
        held = code_ref[point] >= 0

        @pl.when(held)
        def _():
            owned_ref[count] = point

        return count + held.astype(jnp.int32)

    count = lax.fori_loop(0, npoint, scan, jnp.int32(0))

    def fetch(turn):
        row = code_ref[owned_ref[turn]] // grid
        slot = lax.rem(turn, slots)
        return pltpu.make_async_copy(orb_ref.at[:, row, 0, :], buf.at[slot], sem.at[slot])

    def prime(turn, carry):
        fetch(turn).start()
        return carry

    lax.fori_loop(0, jnp.minimum(count, slots - 1), prime, 0)

    def take(turn, carry):
        @pl.when(turn + slots - 1 < count)
        def _():
            fetch(turn + slots - 1).start()

        fetch(turn).wait()
        point = owned_ref[turn]
        lane = lax.rem(code_ref[point], grid)
        hot = (lax.broadcasted_iota(jnp.int32, (8, grid), 1) == lane).astype(f32)
        column = lax.dot_general(
            hot,
            buf[lax.rem(turn, slots)],
            (((1,), (1,)), ((), ())),
            precision=highest,
            preferred_element_type=f32,
        )
        out_ref[pl.ds(point, 1), :] = column[:1]
        return carry

    lax.fori_loop(0, count, take, 0)


def pick(code, orbitals):
    norbit, grid = orbitals.shape[0], orbitals.shape[-1]
    npoint = code.shape[0]
    slots = 16
    return pl.pallas_call(
        functools.partial(pick_kernel, slots),
        out_shape=jax.ShapeDtypeStruct((npoint, norbit), f32),
        in_specs=[
            pl.BlockSpec(memory_space=pltpu.SMEM),
            pl.BlockSpec(memory_space=pl.ANY),
        ],
        out_specs=pl.BlockSpec(memory_space=pltpu.VMEM),
        scratch_shapes=[
            pltpu.SMEM((npoint,), jnp.int32),
            pltpu.VMEM((slots, norbit, grid), f32),
            pltpu.SemaphoreType.DMA((slots,)),
        ],
        compiler_params=pltpu.CompilerParams(vmem_limit_bytes=16 * MIB),
        name="pick_points",
    )(code, orbitals.reshape(norbit, -1, 1, grid))


def solve_kernel(vectors, rows_ref, rows_out, coeff_out, gram_ref, inv_ref):
    npoint = rows_ref.shape[0]
    rows = rows_ref[...]
    high, low = split(rows)
    rows_out[...] = jnp.concatenate([high, high, low], axis=1)
    corr = lax.dot_general(
        rows, rows, (((1,), (1,)), ((), ())), precision=highest, preferred_element_type=f32
    )
    gram = corr * corr
    first = lax.broadcasted_iota(jnp.int32, (npoint, npoint), 0)
    second = lax.broadcasted_iota(jnp.int32, (npoint, npoint), 1)
    eye = (first == second).astype(f32)
    mean = jnp.sum(gram * eye) / npoint
    gram = gram + 0.01 * mean * eye
    scale = 1.0 / jnp.max(jnp.sum(gram, axis=1))
    gram = gram * scale
    gram_ref[...] = gram
    inv_ref[...] = 2.0 * eye - gram

    def residual(inverse):
        ghigh, glow = split(gram_ref[...])
        ihigh, ilow = split(inverse)
        product = mul(ghigh, ihigh) + (mul(ghigh, ilow) + mul(glow, ihigh))
        return eye - product

    def go_on(state):
        turn, size = state
        return (turn < 40) & (size > 1e-5)

    def turn_of(state):
        turn, _ = state
        inverse = inv_ref[...]
        rest = residual(inverse)
        ihigh, ilow = split(inverse)
        rhigh, rlow = split(rest)
        inv_ref[...] = inverse + (mul(ihigh, rhigh) + (mul(ihigh, rlow) + mul(ilow, rhigh)))
        return turn + 1, jnp.sum(rest * rest)

    lax.while_loop(go_on, turn_of, (jnp.int32(0), f32(1.0)))

    target = eye[:vectors]
    inverse = inv_ref[...]

    def exact(left, right):
        return jnp.dot(left, right, precision=highest, preferred_element_type=f32)

    coeff = inverse[:vectors]
    for _ in range(2):
        rest = target - exact(coeff, gram_ref[...])
        coeff = coeff + exact(rest, inverse)
    coeff_out[...] = jnp.concatenate(split(coeff * scale), axis=0)


def solve(rows, vectors):
    npoint, norbit = rows.shape
    return pl.pallas_call(
        functools.partial(solve_kernel, vectors),
        out_shape=[
            jax.ShapeDtypeStruct((npoint, 3 * norbit), bf16),
            jax.ShapeDtypeStruct((2 * vectors, npoint), bf16),
        ],
        in_specs=[pl.BlockSpec(memory_space=pltpu.VMEM)],
        out_specs=[pl.BlockSpec(memory_space=pltpu.VMEM)] * 2,
        scratch_shapes=[
            pltpu.VMEM((npoint, npoint), f32),
            pltpu.VMEM((npoint, npoint), f32),
        ],
        compiler_params=pltpu.CompilerParams(vmem_limit_bytes=40 * MIB),
        name="solve_coeffs",
    )(rows)


def place(wide_count):
    me = lax.axis_index("slab") * wide_count + lax.axis_index("wide")
    return me


def greet(devices, wide_count, me):
    barrier = pltpu.get_barrier_semaphore()

    def signal(offset, carry):
        other = lax.rem(me + offset, devices)
        pl.semaphore_signal(
            barrier,
            inc=1,
            device_id=(other // wide_count, lax.rem(other, wide_count)),
            device_id_type=MESH,
        )
        return carry

    lax.fori_loop(1, devices, signal, 0)
    pl.semaphore_wait(barrier, devices - 1)


def basis(length):
    half = length // 2
    index = np.arange(length)
    freq = np.where(index <= half, index, index - half)
    angle = (index[:, None] * freq[None, :] % length) * (2.0 * math.pi / length)
    edge = (index == 0) | (index == half)
    norm = np.where(edge, math.sqrt(1.0 / length), math.sqrt(2.0 / length))
    table = np.where(index[None, :] <= half, np.cos(angle), np.sin(angle)) * norm[None, :]
    wave = freq.astype(np.float32) * np.float32(2.0 * math.pi / length)
    return table.astype(np.float32), wave * wave


def split_table(table):
    high = table.astype(ml_dtypes.bfloat16)
    low = (table - high.astype(np.float32)).astype(ml_dtypes.bfloat16)
    return high, low


def right_table(table):
    high, low = split_table(table)
    return jnp.asarray(np.block([[high, low], [high, np.zeros_like(high)]]))


def left_table(table):
    high, low = split_table(table)
    return jnp.asarray(np.block([[high, high], [low, np.zeros_like(low)]]))


def times_right(values, table):
    grid = values.shape[1]
    high, low = split(values)
    both = mul(jnp.concatenate([high, low], axis=1), table)
    return both[:, :grid] + both[:, grid:]


def times_left(table, values):
    grid = values.shape[0]
    high, low = split(values)
    both = mul(table, jnp.concatenate([high, low], axis=0))
    return both[:grid] + both[grid:]


def fused_kernel(
    slab_count,
    wide_count,
    steps,
    orb_ref,
    rows_ref,
    coeff_ref,
    rforth_ref,
    rback_ref,
    lforth_ref,
    lback_ref,
    col_ref,
    row_ref,
    out_ref,
    buf,
    work,
    own_sem,
    send_sem,
    recv_sem,
    back_send_sem,
    back_recv_sem,
):
    devices, depth, rows, grid = buf.shape
    norbit, tall, _ = orb_ref.shape
    planes = depth // steps
    step = pl.program_id(0)
    me = place(wide_count)
    slab, wide = lax.axis_index("slab"), lax.axis_index("wide")

    @pl.when(step == 0)
    def _():
        greet(devices, wide_count, me)

    group = math.gcd(tall, 8)

    def block(turn, carry):
        base = turn * group
        cells = jnp.concatenate([orb_ref[:, base + j, :] for j in range(group)], axis=1)
        high, low = split(cells)
        pairs = mul(rows_ref[...], jnp.concatenate([high, low, high], axis=0))
        phigh, plow = split(pairs * pairs)
        main = mul(coeff_ref[...], phigh)
        piece = main[:devices] + (main[devices:] + mul(coeff_ref[:devices], plow))
        first = step * tall + base
        for j in range(group):
            row = first + j
            buf[:, row // rows, lax.rem(row, rows), :] = piece[:, j * grid : (j + 1) * grid]
        return carry

    lax.fori_loop(0, tall // group, block, 0)

    def send(offset, carry):
        other = lax.rem(me + offset, devices)
        pltpu.make_async_remote_copy(
            src_ref=buf.at[other, pl.ds(step * planes, planes)],
            dst_ref=work.at[pl.ds(slab * depth + step * planes, planes), wide],
            send_sem=send_sem,
            recv_sem=recv_sem.at[step],
            device_id=(other // wide_count, lax.rem(other, wide_count)),
            device_id_type=MESH,
        ).start()
        return carry

    lax.fori_loop(1, devices, send, 0)

    @pl.when(step == steps - 1)
    def _():
        transform(
            slab_count,
            wide_count,
            steps,
            rforth_ref,
            rback_ref,
            lforth_ref,
            lback_ref,
            col_ref,
            row_ref,
            out_ref,
            buf,
            work,
            own_sem,
            send_sem,
            recv_sem,
            back_send_sem,
            back_recv_sem,
        )


def transform(
    slab_count,
    wide_count,
    steps,
    rforth_ref,
    rback_ref,
    lforth_ref,
    lback_ref,
    col_ref,
    row_ref,
    out_ref,
    buf,
    work,
    own_sem,
    send_sem,
    recv_sem,
    back_send_sem,
    back_recv_sem,
):
    devices, depth, rows, grid = buf.shape
    planes = depth // steps
    me = place(wide_count)
    slab, wide = lax.axis_index("slab"), lax.axis_index("wide")

    def side_by_side(values):
        return jnp.concatenate(
            [values[j * grid : (j + 1) * grid] for j in range(values.shape[0] // grid)], axis=1
        )

    def stacked(values):
        return jnp.concatenate(
            [values[:, j * grid : (j + 1) * grid] for j in range(values.shape[1] // grid)], axis=0
        )

    def forth(turn, carry):
        arrived = buf.at[pl.ds(0, devices - 1), pl.ds(0, planes)]
        pltpu.make_async_copy(arrived, arrived, recv_sem.at[turn]).wait()
        local = pl.ds(turn * planes, planes)
        work[pl.ds(slab * depth + turn * planes, planes), wide] = buf[me, local]
        places = [pl.ds(at * depth + turn * planes, planes) for at in range(slab_count)]
        values = jnp.concatenate(
            [work[at].reshape(planes * grid, grid) for at in places], axis=0
        )
        along_x = times_right(values, rforth_ref[...])
        along_y = stacked(times_left(lforth_ref[...], side_by_side(along_x)))
        for at in range(slab_count):
            piece = along_y[at * planes * grid : (at + 1) * planes * grid]
            work[places[at]] = piece.reshape(planes, wide_count, rows, grid)
        return carry

    lax.fori_loop(0, steps, forth, 0)

    batch = math.gcd(rows, 8)

    def middle(turn, carry):
        base = turn * batch
        of_wide = base // rows
        of_row = lax.rem(base, rows)
        values = jnp.concatenate(
            [work[:, of_wide, of_row + j, :] for j in range(batch)], axis=1
        )
        spectrum = times_left(lforth_ref[...], values)
        pieces = []
        for j in range(batch):
            yfreq = col_ref[pl.ds(base + j, 1), :]
            total = (col_ref[...] + yfreq) + row_ref[...]
            safe = jnp.where(total > 0, total, 1.0)
            kernel = jnp.where(total > 0, (4.0 * math.pi) / safe, 0.0)
            pieces.append(spectrum[:, j * grid : (j + 1) * grid] * kernel)
        back = times_left(lback_ref[...], jnp.concatenate(pieces, axis=1))
        for j in range(batch):
            work[:, of_wide, of_row + j, :] = back[:, j * grid : (j + 1) * grid]
        return carry

    lax.fori_loop(0, grid // batch, middle, 0)

    others = buf.at[pl.ds(0, devices - 1)]
    pltpu.make_async_copy(others, others, send_sem).wait()
    count = math.gcd(depth, 4)

    def finish(turn, carry):
        to_slab = lax.rem(turn + slab + 1, slab_count)
        inner = (turn // slab_count) * count
        values = work[pl.ds(to_slab * depth + inner, count)].reshape(count * grid, grid)
        along_y = stacked(times_left(lback_ref[...], side_by_side(values)))
        field = times_right(along_y, rback_ref[...]).reshape(count, wide_count, rows, grid)
        for to_wide in range(wide_count):
            buf[to_slab * wide_count + to_wide, pl.ds(inner, count)] = field[:, to_wide]

        def send(offset, inner_carry):
            to_wide = lax.rem(wide + offset, wide_count)

            @pl.when((to_slab != slab) | (to_wide != wide))
            def _():
                pltpu.make_async_remote_copy(
                    src_ref=buf.at[to_slab * wide_count + to_wide, pl.ds(inner, count)],
                    dst_ref=out_ref.at[me, pl.ds(inner, count)],
                    send_sem=back_send_sem,
                    recv_sem=back_recv_sem,
                    device_id=(to_slab, to_wide),
                    device_id_type=MESH,
                ).start()

            return inner_carry

        lax.fori_loop(1, wide_count + 1, send, 0)
        return carry

    lax.fori_loop(0, grid // count, finish, 0)

    mine = pltpu.make_async_copy(buf.at[me], out_ref.at[me], own_sem)
    mine.start()
    mine.wait()
    pltpu.make_async_copy(others, others, back_send_sem).wait()
    pltpu.make_async_copy(others, others, back_recv_sem).wait()


def potentials(orbitals, rows_cat, coeff_cat, slab_count, wide_count):
    norbit, depth, rows, grid = orbitals.shape
    devices = slab_count * wide_count
    tall = max(rows, math.gcd(depth * rows, 32))
    steps = depth * rows // tall
    table, squares = basis(grid)
    tables = [right_table(table), right_table(table.T), left_table(table.T), left_table(table)]
    column = jnp.asarray(np.broadcast_to(squares[:, None], (grid, grid)))
    line = jnp.asarray(squares[None, :])
    vmem = pl.BlockSpec(memory_space=pltpu.VMEM)
    return pl.pallas_call(
        functools.partial(fused_kernel, slab_count, wide_count, steps),
        grid=(steps,),
        out_shape=jax.ShapeDtypeStruct((devices, depth, rows, grid), f32),
        in_specs=[pl.BlockSpec((norbit, tall, grid), lambda step: (0, step, 0))] + [vmem] * 8,
        out_specs=pl.BlockSpec(memory_space=pl.ANY),
        scratch_shapes=[
            pltpu.VMEM((devices, depth, rows, grid), f32),
            pltpu.VMEM((grid, wide_count, rows, grid), f32),
            pltpu.SemaphoreType.DMA,
            pltpu.SemaphoreType.DMA,
            pltpu.SemaphoreType.DMA((steps,)),
            pltpu.SemaphoreType.DMA,
            pltpu.SemaphoreType.DMA,
        ],
        compiler_params=pltpu.CompilerParams(
            collective_id=0, has_side_effects=True, vmem_limit_bytes=56 * MIB
        ),
        name="fit_and_transform",
    )(orbitals.reshape(norbit, depth * rows, grid), rows_cat, coeff_cat, *tables, column, line)


def per_device(orbitals, points):
    norbit, depth, rows, grid = orbitals.shape
    slab_count = lax.axis_size("slab")
    wide_count = lax.axis_size("wide")
    slab_index = lax.axis_index("slab")
    wide_index = lax.axis_index("wide")
    zcoord = points // (grid * grid)
    ycoord = points // grid % grid
    xcoord = points % grid
    owned = (zcoord // depth == slab_index) & (ycoord // rows == wide_index)
    offset = ((zcoord - slab_index * depth) * rows + (ycoord - wide_index * rows)) * grid + xcoord
    code = jnp.where(owned, offset, -1).astype(jnp.int32)
    sampled_rows = lax.psum(pick(code, orbitals), ("slab", "wide"))
    devices = slab_count * wide_count
    rows_cat, coeff_cat = solve(sampled_rows, devices)
    return potentials(orbitals, rows_cat, coeff_cat, slab_count, wide_count)


def solution(mesh):
    placed = (P(None, "slab", "wide", None), P())
    return jax.shard_map(
        per_device,
        mesh=mesh,
        in_specs=placed,
        out_specs=P(None, "slab", "wide", None),
        check_vma=False,
    )
```

```python
import functools
import math

import jax
import jax.numpy as jnp
import ml_dtypes
import numpy as np
from jax import lax
from jax.experimental import pallas as pl
from jax.experimental.pallas import tpu as pltpu
from jax.sharding import PartitionSpec as P

highest = lax.Precision.HIGHEST
MESH = pl.DeviceIdType.MESH
MIB = 1 << 20
f32 = jnp.float32
bf16 = jnp.bfloat16


def split(values):
    high = values.astype(bf16)
    low = (values - high.astype(f32)).astype(bf16)
    return high, low


def mul(left, right):
    return jnp.dot(left, right, preferred_element_type=f32)


def pick_kernel(slots, code_ref, orb_ref, out_ref, owned_ref, buf, sem):
    blocks, norbit, grid = out_ref.shape
    out_ref[...] = jnp.zeros_like(out_ref)

    def scan(point, count):
        owned_ref[count] = point
        return count + (code_ref[point] >= 0).astype(jnp.int32)

    count = lax.fori_loop(0, blocks * grid, scan, jnp.int32(0), unroll=8)

    def fetch(turn):
        row = code_ref[owned_ref[turn]] // grid
        slot = lax.rem(turn, slots)
        return pltpu.make_async_copy(orb_ref.at[:, row, 0, :], buf.at[slot], sem.at[slot])

    def prime(turn, carry):
        fetch(turn).start()
        return carry

    lax.fori_loop(0, jnp.minimum(count, slots - 1), prime, 0)
    lanes = lax.broadcasted_iota(jnp.int32, (norbit, grid), 1)

    def take(turn, carry):
        @pl.when(turn + slots - 1 < count)
        def _():
            fetch(turn + slots - 1).start()

        fetch(turn).wait()
        point = owned_ref[turn]
        lane = lax.rem(code_ref[point], grid)
        target = lax.rem(point, grid)
        moved = pltpu.roll(buf[lax.rem(turn, slots)], lax.rem(target - lane + grid, grid), 1)
        of_block = point // grid
        out_ref[of_block] = jnp.where(lanes == target, moved, out_ref[of_block])
        return carry

    lax.fori_loop(0, count, take, 0)


def pick(code, orbitals):
    norbit, grid = orbitals.shape[0], orbitals.shape[-1]
    npoint = code.shape[0]
    slots = 16
    return pl.pallas_call(
        functools.partial(pick_kernel, slots),
        out_shape=jax.ShapeDtypeStruct((npoint // grid, norbit, grid), f32),
        in_specs=[
            pl.BlockSpec(memory_space=pltpu.SMEM),
            pl.BlockSpec(memory_space=pl.ANY),
        ],
        out_specs=pl.BlockSpec(memory_space=pltpu.VMEM),
        scratch_shapes=[
            pltpu.SMEM((npoint,), jnp.int32),
            pltpu.VMEM((slots, norbit, grid), f32),
            pltpu.SemaphoreType.DMA((slots,)),
        ],
        compiler_params=pltpu.CompilerParams(vmem_limit_bytes=16 * MIB),
        name="pick_points",
    )(code, orbitals.reshape(norbit, -1, 1, grid))


def sum_kernel(wide_count, part_ref, out_ref, parts, whole, sems):
    devices = part_ref.shape[0]
    me = place(wide_count)
    greet(devices, wide_count, me)

    def copy_to(offset, source, target, first):
        other = lax.rem(me + offset, devices)
        pltpu.make_async_remote_copy(
            src_ref=source(other),
            dst_ref=target.at[me],
            send_sem=sems.at[first],
            recv_sem=sems.at[first + 1],
            device_id=(other // wide_count, lax.rem(other, wide_count)),
            device_id_type=MESH,
        ).start()

    def scatter(offset, carry):
        copy_to(offset, lambda other: part_ref.at[other], parts, 0)
        return carry

    def gather(offset, carry):
        copy_to(offset, lambda other: whole.at[me], whole, 2)
        return carry

    lax.fori_loop(1, devices, scatter, 0)
    parts[me] = part_ref[me]
    others = parts.at[pl.ds(0, devices - 1)]
    pltpu.make_async_copy(others, others, sems.at[1]).wait()
    whole[me] = jnp.sum(parts[...], axis=0)
    lax.fori_loop(1, devices, gather, 0)
    pltpu.make_async_copy(others, others, sems.at[3]).wait()
    out_ref[...] = whole[...]
    pltpu.make_async_copy(others, others, sems.at[0]).wait()
    pltpu.make_async_copy(others, others, sems.at[2]).wait()


def sum_over(picked, slab_count, wide_count):
    devices = slab_count * wide_count
    grid = picked.shape[-1]
    shape = (devices, picked.size // (devices * grid), grid)
    vmem = pl.BlockSpec(memory_space=pltpu.VMEM)
    total = pl.pallas_call(
        functools.partial(sum_kernel, wide_count),
        out_shape=jax.ShapeDtypeStruct(shape, f32),
        in_specs=[vmem],
        out_specs=vmem,
        scratch_shapes=[
            pltpu.VMEM(shape, f32),
            pltpu.VMEM(shape, f32),
            pltpu.SemaphoreType.DMA((4,)),
        ],
        compiler_params=pltpu.CompilerParams(
            collective_id=1, has_side_effects=True, vmem_limit_bytes=16 * MIB
        ),
        name="sum_picked",
    )(picked.reshape(shape))
    return total.reshape(picked.shape)


def solve_kernel(vectors, rows_ref, rows_out, coeff_out, gram_ref, inv_ref):
    npoint = gram_ref.shape[0]
    rows = jnp.concatenate([rows_ref[at] for at in range(rows_ref.shape[0])], axis=1).T
    high, low = split(rows)
    rows_out[...] = jnp.concatenate([high, high, low], axis=1)
    corr = lax.dot_general(
        rows, rows, (((1,), (1,)), ((), ())), precision=highest, preferred_element_type=f32
    )
    gram = corr * corr
    first = lax.broadcasted_iota(jnp.int32, (npoint, npoint), 0)
    second = lax.broadcasted_iota(jnp.int32, (npoint, npoint), 1)
    eye = (first == second).astype(f32)
    mean = jnp.sum(gram * eye) / npoint
    gram = gram + 0.01 * mean * eye
    scale = 1.0 / jnp.max(jnp.sum(gram, axis=1))
    gram = gram * scale
    gram_ref[...] = gram
    inv_ref[...] = 2.0 * eye - gram

    def residual(inverse):
        ghigh, glow = split(gram_ref[...])
        ihigh, ilow = split(inverse)
        product = mul(ghigh, ihigh) + (mul(ghigh, ilow) + mul(glow, ihigh))
        return eye - product

    def go_on(state):
        turn, size = state
        return (turn < 40) & (size > 1e-5)

    def turn_of(state):
        turn, _ = state
        inverse = inv_ref[...]
        rest = residual(inverse)
        ihigh, ilow = split(inverse)
        rhigh, rlow = split(rest)
        inv_ref[...] = inverse + (mul(ihigh, rhigh) + (mul(ihigh, rlow) + mul(ilow, rhigh)))
        return turn + 1, jnp.sum(rest * rest)

    lax.while_loop(go_on, turn_of, (jnp.int32(0), f32(1.0)))

    target = eye[:vectors]
    inverse = inv_ref[...]

    def exact(left, right):
        return jnp.dot(left, right, precision=highest, preferred_element_type=f32)

    coeff = inverse[:vectors]
    for _ in range(2):
        rest = target - exact(coeff, gram_ref[...])
        coeff = coeff + exact(rest, inverse)
    coeff_out[...] = jnp.concatenate(split(coeff * scale), axis=0)


def solve(rows, vectors):
    blocks, norbit, grid = rows.shape
    npoint = blocks * grid
    return pl.pallas_call(
        functools.partial(solve_kernel, vectors),
        out_shape=[
            jax.ShapeDtypeStruct((npoint, 3 * norbit), bf16),
            jax.ShapeDtypeStruct((2 * vectors, npoint), bf16),
        ],
        in_specs=[pl.BlockSpec(memory_space=pltpu.VMEM)],
        out_specs=[pl.BlockSpec(memory_space=pltpu.VMEM)] * 2,
        scratch_shapes=[
            pltpu.VMEM((npoint, npoint), f32),
            pltpu.VMEM((npoint, npoint), f32),
        ],
        compiler_params=pltpu.CompilerParams(vmem_limit_bytes=40 * MIB),
        name="solve_coeffs",
    )(rows)


def place(wide_count):
    me = lax.axis_index("slab") * wide_count + lax.axis_index("wide")
    return me


def greet(devices, wide_count, me):
    barrier = pltpu.get_barrier_semaphore()

    def signal(offset, carry):
        other = lax.rem(me + offset, devices)
        pl.semaphore_signal(
            barrier,
            inc=1,
            device_id=(other // wide_count, lax.rem(other, wide_count)),
            device_id_type=MESH,
        )
        return carry

    lax.fori_loop(1, devices, signal, 0)
    pl.semaphore_wait(barrier, devices - 1)


def basis(length):
    half = length // 2
    index = np.arange(length)
    freq = np.where(index <= half, index, index - half)
    angle = (index[:, None] * freq[None, :] % length) * (2.0 * math.pi / length)
    edge = (index == 0) | (index == half)
    norm = np.where(edge, math.sqrt(1.0 / length), math.sqrt(2.0 / length))
    table = np.where(index[None, :] <= half, np.cos(angle), np.sin(angle)) * norm[None, :]
    wave = freq.astype(np.float32) * np.float32(2.0 * math.pi / length)
    return table.astype(np.float32), wave * wave


def split_table(table):
    high = table.astype(ml_dtypes.bfloat16)
    low = (table - high.astype(np.float32)).astype(ml_dtypes.bfloat16)
    return high, low


def right_table(table):
    high, low = split_table(table)
    return jnp.asarray(np.block([[high, low], [high, np.zeros_like(high)]]))


def left_table(table):
    high, low = split_table(table)
    return jnp.asarray(np.block([[high, high], [low, np.zeros_like(low)]]))


def times_right(values, table):
    grid = values.shape[1]
    high, low = split(values)
    both = mul(jnp.concatenate([high, low], axis=1), table)
    return both[:, :grid] + both[:, grid:]


def times_left(table, values):
    grid = values.shape[0]
    high, low = split(values)
    both = mul(table, jnp.concatenate([high, low], axis=0))
    return both[:grid] + both[grid:]


def fused_kernel(
    slab_count,
    wide_count,
    steps,
    orb_ref,
    rows_ref,
    coeff_ref,
    rforth_ref,
    rback_ref,
    lforth_ref,
    lback_ref,
    col_ref,
    row_ref,
    out_ref,
    buf,
    work,
    own_sem,
    send_sem,
    recv_sem,
    back_send_sem,
    back_recv_sem,
):
    devices, depth, rows, grid = buf.shape
    norbit, tall, _ = orb_ref.shape
    planes = depth // steps
    step = pl.program_id(0)
    me = place(wide_count)
    slab, wide = lax.axis_index("slab"), lax.axis_index("wide")

    @pl.when(step == 0)
    def _():
        greet(devices, wide_count, me)

    group = math.gcd(tall, 8)

    def block(turn, carry):
        base = turn * group
        cells = jnp.concatenate([orb_ref[:, base + j, :] for j in range(group)], axis=1)
        high, low = split(cells)
        pairs = mul(rows_ref[...], jnp.concatenate([high, low, high], axis=0))
        phigh, plow = split(pairs * pairs)
        main = mul(coeff_ref[...], phigh)
        piece = main[:devices] + (main[devices:] + mul(coeff_ref[:devices], plow))
        first = step * tall + base
        for j in range(group):
            row = first + j
            buf[:, row // rows, lax.rem(row, rows), :] = piece[:, j * grid : (j + 1) * grid]
        return carry

    lax.fori_loop(0, tall // group, block, 0)

    def send(offset, carry):
        other = lax.rem(me + offset, devices)
        pltpu.make_async_remote_copy(
            src_ref=buf.at[other, pl.ds(step * planes, planes)],
            dst_ref=work.at[pl.ds(slab * depth + step * planes, planes), wide],
            send_sem=send_sem,
            recv_sem=recv_sem.at[step],
            device_id=(other // wide_count, lax.rem(other, wide_count)),
            device_id_type=MESH,
        ).start()
        return carry

    lax.fori_loop(1, devices, send, 0)

    @pl.when(step == steps - 1)
    def _():
        transform(
            slab_count,
            wide_count,
            steps,
            rforth_ref,
            rback_ref,
            lforth_ref,
            lback_ref,
            col_ref,
            row_ref,
            out_ref,
            buf,
            work,
            own_sem,
            send_sem,
            recv_sem,
            back_send_sem,
            back_recv_sem,
        )


def transform(
    slab_count,
    wide_count,
    steps,
    rforth_ref,
    rback_ref,
    lforth_ref,
    lback_ref,
    col_ref,
    row_ref,
    out_ref,
    buf,
    work,
    own_sem,
    send_sem,
    recv_sem,
    back_send_sem,
    back_recv_sem,
):
    devices, depth, rows, grid = buf.shape
    planes = depth // steps
    me = place(wide_count)
    slab, wide = lax.axis_index("slab"), lax.axis_index("wide")

    def side_by_side(values):
        return jnp.concatenate(
            [values[j * grid : (j + 1) * grid] for j in range(values.shape[0] // grid)], axis=1
        )

    def stacked(values):
        return jnp.concatenate(
            [values[:, j * grid : (j + 1) * grid] for j in range(values.shape[1] // grid)], axis=0
        )

    def forth(turn, carry):
        arrived = buf.at[pl.ds(0, devices - 1), pl.ds(0, planes)]
        pltpu.make_async_copy(arrived, arrived, recv_sem.at[turn]).wait()
        local = pl.ds(turn * planes, planes)
        work[pl.ds(slab * depth + turn * planes, planes), wide] = buf[me, local]
        places = [pl.ds(at * depth + turn * planes, planes) for at in range(slab_count)]
        values = jnp.concatenate(
            [work[at].reshape(planes * grid, grid) for at in places], axis=0
        )
        along_x = times_right(values, rforth_ref[...])
        along_y = stacked(times_left(lforth_ref[...], side_by_side(along_x)))
        for at in range(slab_count):
            piece = along_y[at * planes * grid : (at + 1) * planes * grid]
            work[places[at]] = piece.reshape(planes, wide_count, rows, grid)
        return carry

    lax.fori_loop(0, steps, forth, 0)

    batch = math.gcd(rows, 8)

    def middle(turn, carry):
        base = turn * batch
        of_wide = base // rows
        of_row = lax.rem(base, rows)
        values = jnp.concatenate(
            [work[:, of_wide, of_row + j, :] for j in range(batch)], axis=1
        )
        spectrum = times_left(lforth_ref[...], values)
        pieces = []
        for j in range(batch):
            yfreq = col_ref[pl.ds(base + j, 1), :]
            total = (col_ref[...] + yfreq) + row_ref[...]
            safe = jnp.where(total > 0, total, 1.0)
            kernel = jnp.where(total > 0, (4.0 * math.pi) / safe, 0.0)
            pieces.append(spectrum[:, j * grid : (j + 1) * grid] * kernel)
        back = times_left(lback_ref[...], jnp.concatenate(pieces, axis=1))
        for j in range(batch):
            work[:, of_wide, of_row + j, :] = back[:, j * grid : (j + 1) * grid]
        return carry

    lax.fori_loop(0, grid // batch, middle, 0)

    others = buf.at[pl.ds(0, devices - 1)]
    pltpu.make_async_copy(others, others, send_sem).wait()
    count = math.gcd(depth, 4)

    def finish(turn, carry):
        to_slab = lax.rem(turn + slab + 1, slab_count)
        inner = (turn // slab_count) * count
        values = work[pl.ds(to_slab * depth + inner, count)].reshape(count * grid, grid)
        along_y = stacked(times_left(lback_ref[...], side_by_side(values)))
        field = times_right(along_y, rback_ref[...]).reshape(count, wide_count, rows, grid)
        for to_wide in range(wide_count):
            buf[to_slab * wide_count + to_wide, pl.ds(inner, count)] = field[:, to_wide]

        def send(offset, inner_carry):
            to_wide = lax.rem(wide + offset, wide_count)

            @pl.when((to_slab != slab) | (to_wide != wide))
            def _():
                pltpu.make_async_remote_copy(
                    src_ref=buf.at[to_slab * wide_count + to_wide, pl.ds(inner, count)],
                    dst_ref=out_ref.at[me, pl.ds(inner, count)],
                    send_sem=back_send_sem,
                    recv_sem=back_recv_sem,
                    device_id=(to_slab, to_wide),
                    device_id_type=MESH,
                ).start()

            return inner_carry

        lax.fori_loop(1, wide_count + 1, send, 0)
        return carry

    lax.fori_loop(0, grid // count, finish, 0)

    mine = pltpu.make_async_copy(buf.at[me], out_ref.at[me], own_sem)
    mine.start()
    mine.wait()
    pltpu.make_async_copy(others, others, back_send_sem).wait()
    pltpu.make_async_copy(others, others, back_recv_sem).wait()


def potentials(orbitals, rows_cat, coeff_cat, slab_count, wide_count):
    norbit, depth, rows, grid = orbitals.shape
    devices = slab_count * wide_count
    tall = max(rows, math.gcd(depth * rows, 32))
    steps = depth * rows // tall
    table, squares = basis(grid)
    tables = [right_table(table), right_table(table.T), left_table(table.T), left_table(table)]
    column = jnp.asarray(np.broadcast_to(squares[:, None], (grid, grid)))
    line = jnp.asarray(squares[None, :])
    vmem = pl.BlockSpec(memory_space=pltpu.VMEM)
    return pl.pallas_call(
        functools.partial(fused_kernel, slab_count, wide_count, steps),
        grid=(steps,),
        out_shape=jax.ShapeDtypeStruct((devices, depth, rows, grid), f32),
        in_specs=[pl.BlockSpec((norbit, tall, grid), lambda step: (0, step, 0))] + [vmem] * 8,
        out_specs=pl.BlockSpec(memory_space=pl.ANY),
        scratch_shapes=[
            pltpu.VMEM((devices, depth, rows, grid), f32),
            pltpu.VMEM((grid, wide_count, rows, grid), f32),
            pltpu.SemaphoreType.DMA,
            pltpu.SemaphoreType.DMA,
            pltpu.SemaphoreType.DMA((steps,)),
            pltpu.SemaphoreType.DMA,
            pltpu.SemaphoreType.DMA,
        ],
        compiler_params=pltpu.CompilerParams(
            collective_id=0, has_side_effects=True, vmem_limit_bytes=56 * MIB
        ),
        name="fit_and_transform",
    )(orbitals.reshape(norbit, depth * rows, grid), rows_cat, coeff_cat, *tables, column, line)


def per_device(orbitals, points):
    norbit, depth, rows, grid = orbitals.shape
    slab_count = lax.axis_size("slab")
    wide_count = lax.axis_size("wide")
    slab_index = lax.axis_index("slab")
    wide_index = lax.axis_index("wide")
    zcoord = points // (grid * grid)
    ycoord = points // grid % grid
    xcoord = points % grid
    owned = (zcoord // depth == slab_index) & (ycoord // rows == wide_index)
    offset = ((zcoord - slab_index * depth) * rows + (ycoord - wide_index * rows)) * grid + xcoord
    code = jnp.where(owned, offset, -1).astype(jnp.int32)
    sampled = sum_over(pick(code, orbitals), slab_count, wide_count)
    rows_cat, coeff_cat = solve(sampled, slab_count * wide_count)
    return potentials(orbitals, rows_cat, coeff_cat, slab_count, wide_count)


def solution(mesh):
    placed = (P(None, "slab", "wide", None), P())
    return jax.shard_map(
        per_device,
        mesh=mesh,
        in_specs=placed,
        out_specs=P(None, "slab", "wide", None),
        check_vma=False,
    )
```

```python
import functools
import math

import jax
import jax.numpy as jnp
import ml_dtypes
import numpy as np
from jax import lax
from jax.experimental import pallas as pl
from jax.experimental.pallas import tpu as pltpu
from jax.sharding import PartitionSpec as P

highest = lax.Precision.HIGHEST
MESH = pl.DeviceIdType.MESH
MIB = 1 << 20
f32 = jnp.float32
bf16 = jnp.bfloat16


def split(values):
    high = values.astype(bf16)
    low = (values - high.astype(f32)).astype(bf16)
    return high, low


def mul(left, right):
    return jnp.dot(left, right, preferred_element_type=f32)


def pick_kernel(slots, code_ref, orb_ref, out_ref, owned_ref, buf, sem):
    blocks, norbit, grid = out_ref.shape
    out_ref[...] = jnp.zeros_like(out_ref)

    def scan(point, count):
        owned_ref[count] = point
        return count + (code_ref[point] >= 0).astype(jnp.int32)

    count = lax.fori_loop(0, blocks * grid, scan, jnp.int32(0), unroll=8)

    def fetch(turn):
        row = code_ref[owned_ref[turn]] // grid
        slot = lax.rem(turn, slots)
        return pltpu.make_async_copy(orb_ref.at[:, row, 0, :], buf.at[slot], sem.at[slot])

    def prime(turn, carry):
        fetch(turn).start()
        return carry

    lax.fori_loop(0, jnp.minimum(count, slots - 1), prime, 0)
    lanes = lax.broadcasted_iota(jnp.int32, (norbit, grid), 1)

    def take(turn, carry):
        @pl.when(turn + slots - 1 < count)
        def _():
            fetch(turn + slots - 1).start()

        fetch(turn).wait()
        point = owned_ref[turn]
        lane = lax.rem(code_ref[point], grid)
        target = lax.rem(point, grid)
        moved = pltpu.roll(buf[lax.rem(turn, slots)], lax.rem(target - lane + grid, grid), 1)
        of_block = point // grid
        out_ref[of_block] = jnp.where(lanes == target, moved, out_ref[of_block])
        return carry

    lax.fori_loop(0, count, take, 0)


def pick(code, orbitals):
    norbit, grid = orbitals.shape[0], orbitals.shape[-1]
    npoint = code.shape[0]
    slots = 16
    return pl.pallas_call(
        functools.partial(pick_kernel, slots),
        out_shape=jax.ShapeDtypeStruct((npoint // grid, norbit, grid), f32),
        in_specs=[
            pl.BlockSpec(memory_space=pltpu.SMEM),
            pl.BlockSpec(memory_space=pl.ANY),
        ],
        out_specs=pl.BlockSpec(memory_space=pltpu.VMEM),
        scratch_shapes=[
            pltpu.SMEM((npoint,), jnp.int32),
            pltpu.VMEM((slots, norbit, grid), f32),
            pltpu.SemaphoreType.DMA((slots,)),
        ],
        compiler_params=pltpu.CompilerParams(vmem_limit_bytes=16 * MIB),
        name="pick_points",
    )(code, orbitals.reshape(norbit, -1, 1, grid))


def sum_kernel(wide_count, part_ref, out_ref, parts, whole, sems):
    devices = part_ref.shape[0]
    me = place(wide_count)
    greet(devices, wide_count, me)

    def copy_to(offset, source, target, first):
        other = lax.rem(me + offset, devices)
        pltpu.make_async_remote_copy(
            src_ref=source(other),
            dst_ref=target.at[me],
            send_sem=sems.at[first],
            recv_sem=sems.at[first + 1],
            device_id=(other // wide_count, lax.rem(other, wide_count)),
            device_id_type=MESH,
        ).start()

    def scatter(offset, carry):
        copy_to(offset, lambda other: part_ref.at[other], parts, 0)
        return carry

    def gather(offset, carry):
        copy_to(offset, lambda other: whole.at[me], whole, 2)
        return carry

    lax.fori_loop(1, devices, scatter, 0)
    parts[me] = part_ref[me]
    others = parts.at[pl.ds(0, devices - 1)]
    pltpu.make_async_copy(others, others, sems.at[1]).wait()
    whole[me] = jnp.sum(parts[...], axis=0)
    lax.fori_loop(1, devices, gather, 0)
    pltpu.make_async_copy(others, others, sems.at[3]).wait()
    out_ref[...] = whole[...]
    pltpu.make_async_copy(others, others, sems.at[0]).wait()
    pltpu.make_async_copy(others, others, sems.at[2]).wait()


def sum_over(picked, slab_count, wide_count):
    devices = slab_count * wide_count
    grid = picked.shape[-1]
    shape = (devices, picked.size // (devices * grid), grid)
    vmem = pl.BlockSpec(memory_space=pltpu.VMEM)
    total = pl.pallas_call(
        functools.partial(sum_kernel, wide_count),
        out_shape=jax.ShapeDtypeStruct(shape, f32),
        in_specs=[vmem],
        out_specs=vmem,
        scratch_shapes=[
            pltpu.VMEM(shape, f32),
            pltpu.VMEM(shape, f32),
            pltpu.SemaphoreType.DMA((4,)),
        ],
        compiler_params=pltpu.CompilerParams(
            collective_id=1, has_side_effects=True, vmem_limit_bytes=16 * MIB
        ),
        name="sum_picked",
    )(picked.reshape(shape))
    return total.reshape(picked.shape)


def solve_kernel(vectors, rows_ref, rows_out, coeff_out, gram_ref, inv_ref):
    npoint = gram_ref.shape[0]
    rows = jnp.concatenate([rows_ref[at] for at in range(rows_ref.shape[0])], axis=1).T
    high, low = split(rows)
    rows_out[...] = jnp.concatenate([high, high, low], axis=1)
    corr = lax.dot_general(
        rows, rows, (((1,), (1,)), ((), ())), precision=highest, preferred_element_type=f32
    )
    gram = corr * corr
    first = lax.broadcasted_iota(jnp.int32, (npoint, npoint), 0)
    second = lax.broadcasted_iota(jnp.int32, (npoint, npoint), 1)
    eye = (first == second).astype(f32)
    mean = jnp.sum(gram * eye) / npoint
    gram = gram + 0.01 * mean * eye
    scale = 1.0 / jnp.max(jnp.sum(gram, axis=1))
    gram = gram * scale
    gram_ref[...] = gram
    inv_ref[...] = 2.0 * eye - gram

    def residual(inverse):
        ghigh, glow = split(gram_ref[...])
        ihigh, ilow = split(inverse)
        product = mul(ghigh, ihigh) + (mul(ghigh, ilow) + mul(glow, ihigh))
        return eye - product

    def go_on(state):
        turn, size = state
        return (turn < 40) & (size > 1e-5)

    def turn_of(state):
        turn, _ = state
        inverse = inv_ref[...]
        rest = residual(inverse)
        ihigh, ilow = split(inverse)
        rhigh, rlow = split(rest)
        inv_ref[...] = inverse + (mul(ihigh, rhigh) + (mul(ihigh, rlow) + mul(ilow, rhigh)))
        return turn + 1, jnp.sum(rest * rest)

    lax.while_loop(go_on, turn_of, (jnp.int32(0), f32(1.0)))

    target = eye[:vectors]
    inverse = inv_ref[...]

    def exact(left, right):
        return jnp.dot(left, right, precision=highest, preferred_element_type=f32)

    coeff = inverse[:vectors]
    for _ in range(2):
        rest = target - exact(coeff, gram_ref[...])
        coeff = coeff + exact(rest, inverse)
    coeff_out[...] = jnp.concatenate(split(coeff * scale), axis=0)


def solve(rows, vectors):
    blocks, norbit, grid = rows.shape
    npoint = blocks * grid
    return pl.pallas_call(
        functools.partial(solve_kernel, vectors),
        out_shape=[
            jax.ShapeDtypeStruct((npoint, 3 * norbit), bf16),
            jax.ShapeDtypeStruct((2 * vectors, npoint), bf16),
        ],
        in_specs=[pl.BlockSpec(memory_space=pltpu.VMEM)],
        out_specs=[pl.BlockSpec(memory_space=pltpu.VMEM)] * 2,
        scratch_shapes=[
            pltpu.VMEM((npoint, npoint), f32),
            pltpu.VMEM((npoint, npoint), f32),
        ],
        compiler_params=pltpu.CompilerParams(vmem_limit_bytes=40 * MIB),
        name="solve_coeffs",
    )(rows)


def place(wide_count):
    me = lax.axis_index("slab") * wide_count + lax.axis_index("wide")
    return me


def greet(devices, wide_count, me):
    barrier = pltpu.get_barrier_semaphore()

    def signal(offset, carry):
        other = lax.rem(me + offset, devices)
        pl.semaphore_signal(
            barrier,
            inc=1,
            device_id=(other // wide_count, lax.rem(other, wide_count)),
            device_id_type=MESH,
        )
        return carry

    lax.fori_loop(1, devices, signal, 0)
    pl.semaphore_wait(barrier, devices - 1)


def basis(length):
    half = length // 2
    index = np.arange(length)
    freq = np.where(index <= half, index, index - half)
    angle = (index[:, None] * freq[None, :] % length) * (2.0 * math.pi / length)
    edge = (index == 0) | (index == half)
    norm = np.where(edge, math.sqrt(1.0 / length), math.sqrt(2.0 / length))
    table = np.where(index[None, :] <= half, np.cos(angle), np.sin(angle)) * norm[None, :]
    wave = freq.astype(np.float32) * np.float32(2.0 * math.pi / length)
    return table.astype(np.float32), wave * wave


def split_table(table):
    high = table.astype(ml_dtypes.bfloat16)
    low = (table - high.astype(np.float32)).astype(ml_dtypes.bfloat16)
    return high, low


def right_table(table):
    high, low = split_table(table)
    return jnp.asarray(np.block([[high, low], [high, np.zeros_like(high)]]))


def left_table(table):
    high, low = split_table(table)
    return jnp.asarray(np.block([[high, high], [low, np.zeros_like(low)]]))


def times_right(values, table):
    grid = values.shape[1]
    high, low = split(values)
    both = mul(jnp.concatenate([high, low], axis=1), table)
    return both[:, :grid] + both[:, grid:]


def times_left(table, values):
    grid = values.shape[0]
    high, low = split(values)
    both = mul(table, jnp.concatenate([high, low], axis=0))
    return both[:grid] + both[grid:]


def fused_kernel(
    slab_count,
    wide_count,
    steps,
    orb_ref,
    rows_ref,
    coeff_ref,
    rforth_ref,
    rback_ref,
    lforth_ref,
    lback_ref,
    col_ref,
    row_ref,
    out_ref,
    buf,
    work,
    own_sem,
    send_sem,
    recv_sem,
    back_send_sem,
    back_recv_sem,
):
    devices, depth, rows, grid = buf.shape
    norbit, tall, _ = orb_ref.shape
    planes = depth // steps
    step = pl.program_id(0)
    me = place(wide_count)
    slab, wide = lax.axis_index("slab"), lax.axis_index("wide")

    @pl.when(step == 0)
    def _():
        greet(devices, wide_count, me)

    group = math.gcd(tall, 8)

    def block(turn, carry):
        base = turn * group
        cells = jnp.concatenate([orb_ref[:, base + j, :] for j in range(group)], axis=1)
        high, low = split(cells)
        pairs = mul(rows_ref[...], jnp.concatenate([high, low, high], axis=0))
        phigh, plow = split(pairs * pairs)
        main = mul(coeff_ref[...], phigh)
        piece = main[:devices] + (main[devices:] + mul(coeff_ref[:devices], plow))
        first = step * tall + base
        for j in range(group):
            row = first + j
            buf[:, row // rows, lax.rem(row, rows), :] = piece[:, j * grid : (j + 1) * grid]
        return carry

    lax.fori_loop(0, tall // group, block, 0)

    lag = steps // 4

    def send_step(which, parity):
        def send(offset, carry):
            other = lax.rem(me + offset, devices)

            @pl.when(lax.rem(other // wide_count, 2) == parity)
            def _():
                pltpu.make_async_remote_copy(
                    src_ref=buf.at[other, pl.ds(which * planes, planes)],
                    dst_ref=work.at[pl.ds(slab * depth + which * planes, planes), wide],
                    send_sem=send_sem,
                    recv_sem=recv_sem.at[which],
                    device_id=(other // wide_count, lax.rem(other, wide_count)),
                    device_id_type=MESH,
                ).start()

            return carry

        lax.fori_loop(1, devices, send, 0)

    send_step(step, 0)

    @pl.when(step >= lag)
    def _():
        send_step(step - lag, 1)

    @pl.when(step == steps - 1)
    def _():
        def send_late(which, carry):
            send_step(which, 1)
            return carry

        lax.fori_loop(steps - lag, steps, send_late, 0)
        transform(
            slab_count,
            wide_count,
            steps,
            rforth_ref,
            rback_ref,
            lforth_ref,
            lback_ref,
            col_ref,
            row_ref,
            out_ref,
            buf,
            work,
            own_sem,
            send_sem,
            recv_sem,
            back_send_sem,
            back_recv_sem,
        )


def transform(
    slab_count,
    wide_count,
    steps,
    rforth_ref,
    rback_ref,
    lforth_ref,
    lback_ref,
    col_ref,
    row_ref,
    out_ref,
    buf,
    work,
    own_sem,
    send_sem,
    recv_sem,
    back_send_sem,
    back_recv_sem,
):
    devices, depth, rows, grid = buf.shape
    planes = depth // steps
    me = place(wide_count)
    slab, wide = lax.axis_index("slab"), lax.axis_index("wide")

    def side_by_side(values):
        return jnp.concatenate(
            [values[j * grid : (j + 1) * grid] for j in range(values.shape[0] // grid)], axis=1
        )

    def stacked(values):
        return jnp.concatenate(
            [values[:, j * grid : (j + 1) * grid] for j in range(values.shape[1] // grid)], axis=0
        )

    def forth(turn, carry):
        arrived = buf.at[pl.ds(0, devices - 1), pl.ds(0, planes)]
        pltpu.make_async_copy(arrived, arrived, recv_sem.at[turn]).wait()
        local = pl.ds(turn * planes, planes)
        work[pl.ds(slab * depth + turn * planes, planes), wide] = buf[me, local]
        places = [pl.ds(at * depth + turn * planes, planes) for at in range(slab_count)]
        values = jnp.concatenate(
            [work[at].reshape(planes * grid, grid) for at in places], axis=0
        )
        along_x = times_right(values, rforth_ref[...])
        along_y = stacked(times_left(lforth_ref[...], side_by_side(along_x)))
        for at in range(slab_count):
            piece = along_y[at * planes * grid : (at + 1) * planes * grid]
            work[places[at]] = piece.reshape(planes, wide_count, rows, grid)
        return carry

    lax.fori_loop(0, steps, forth, 0)

    batch = math.gcd(rows, 8)

    def middle(turn, carry):
        base = turn * batch
        of_wide = base // rows
        of_row = lax.rem(base, rows)
        values = jnp.concatenate(
            [work[:, of_wide, of_row + j, :] for j in range(batch)], axis=1
        )
        spectrum = times_left(lforth_ref[...], values)
        pieces = []
        for j in range(batch):
            yfreq = col_ref[pl.ds(base + j, 1), :]
            total = (col_ref[...] + yfreq) + row_ref[...]
            safe = jnp.where(total > 0, total, 1.0)
            kernel = jnp.where(total > 0, (4.0 * math.pi) / safe, 0.0)
            pieces.append(spectrum[:, j * grid : (j + 1) * grid] * kernel)
        back = times_left(lback_ref[...], jnp.concatenate(pieces, axis=1))
        for j in range(batch):
            work[:, of_wide, of_row + j, :] = back[:, j * grid : (j + 1) * grid]
        return carry

    lax.fori_loop(0, grid // batch, middle, 0)

    others = buf.at[pl.ds(0, devices - 1)]
    pltpu.make_async_copy(others, others, send_sem).wait()
    count = math.gcd(depth, 4)

    def finish(turn, carry):
        to_slab = lax.rem(turn + slab + 1, slab_count)
        inner = (turn // slab_count) * count
        values = work[pl.ds(to_slab * depth + inner, count)].reshape(count * grid, grid)
        along_y = stacked(times_left(lback_ref[...], side_by_side(values)))
        field = times_right(along_y, rback_ref[...]).reshape(count, wide_count, rows, grid)
        for to_wide in range(wide_count):
            buf[to_slab * wide_count + to_wide, pl.ds(inner, count)] = field[:, to_wide]

        def send(offset, inner_carry):
            to_wide = lax.rem(wide + offset, wide_count)

            @pl.when((to_slab != slab) | (to_wide != wide))
            def _():
                pltpu.make_async_remote_copy(
                    src_ref=buf.at[to_slab * wide_count + to_wide, pl.ds(inner, count)],
                    dst_ref=out_ref.at[me, pl.ds(inner, count)],
                    send_sem=back_send_sem,
                    recv_sem=back_recv_sem,
                    device_id=(to_slab, to_wide),
                    device_id_type=MESH,
                ).start()

            return inner_carry

        lax.fori_loop(1, wide_count + 1, send, 0)
        return carry

    lax.fori_loop(0, grid // count, finish, 0)

    mine = pltpu.make_async_copy(buf.at[me], out_ref.at[me], own_sem)
    mine.start()
    mine.wait()
    pltpu.make_async_copy(others, others, back_send_sem).wait()
    pltpu.make_async_copy(others, others, back_recv_sem).wait()


def potentials(orbitals, rows_cat, coeff_cat, slab_count, wide_count):
    norbit, depth, rows, grid = orbitals.shape
    devices = slab_count * wide_count
    tall = max(rows, math.gcd(depth * rows, 32))
    steps = depth * rows // tall
    table, squares = basis(grid)
    tables = [right_table(table), right_table(table.T), left_table(table.T), left_table(table)]
    column = jnp.asarray(np.broadcast_to(squares[:, None], (grid, grid)))
    line = jnp.asarray(squares[None, :])
    vmem = pl.BlockSpec(memory_space=pltpu.VMEM)
    return pl.pallas_call(
        functools.partial(fused_kernel, slab_count, wide_count, steps),
        grid=(steps,),
        out_shape=jax.ShapeDtypeStruct((devices, depth, rows, grid), f32),
        in_specs=[pl.BlockSpec((norbit, tall, grid), lambda step: (0, step, 0))] + [vmem] * 8,
        out_specs=pl.BlockSpec(memory_space=pl.ANY),
        scratch_shapes=[
            pltpu.VMEM((devices, depth, rows, grid), f32),
            pltpu.VMEM((grid, wide_count, rows, grid), f32),
            pltpu.SemaphoreType.DMA,
            pltpu.SemaphoreType.DMA,
            pltpu.SemaphoreType.DMA((steps,)),
            pltpu.SemaphoreType.DMA,
            pltpu.SemaphoreType.DMA,
        ],
        compiler_params=pltpu.CompilerParams(
            collective_id=0, has_side_effects=True, vmem_limit_bytes=56 * MIB
        ),
        name="fit_and_transform",
    )(orbitals.reshape(norbit, depth * rows, grid), rows_cat, coeff_cat, *tables, column, line)


def per_device(orbitals, points):
    norbit, depth, rows, grid = orbitals.shape
    slab_count = lax.axis_size("slab")
    wide_count = lax.axis_size("wide")
    slab_index = lax.axis_index("slab")
    wide_index = lax.axis_index("wide")
    zcoord = points // (grid * grid)
    ycoord = points // grid % grid
    xcoord = points % grid
    owned = (zcoord // depth == slab_index) & (ycoord // rows == wide_index)
    offset = ((zcoord - slab_index * depth) * rows + (ycoord - wide_index * rows)) * grid + xcoord
    code = jnp.where(owned, offset, -1).astype(jnp.int32)
    sampled = sum_over(pick(code, orbitals), slab_count, wide_count)
    rows_cat, coeff_cat = solve(sampled, slab_count * wide_count)
    return potentials(orbitals, rows_cat, coeff_cat, slab_count, wide_count)


def solution(mesh):
    placed = (P(None, "slab", "wide", None), P())
    return jax.shard_map(
        per_device,
        mesh=mesh,
        in_specs=placed,
        out_specs=P(None, "slab", "wide", None),
        check_vma=False,
    )
```
